512 devices in a mesh: row: 32 (over z, x), col: 16 (over y, core).
Axes of the slice: x: 4, y: 8, z: 8, core: 2. Of those that a mesh axis runs over, the one named last changes fastest.
Arguments:
- pair: bfloat16 [512, 512, 128], P('row', 'col'), may hold values from -6 to 6
- gain_in: float32 [128], replicated, may hold values from 0.5 to 2
- w_in: bfloat16 [128, 512], replicated, may hold values from -0.5 to 0.5
- w_gate: bfloat16 [128, 128], replicated, may hold values from -0.5 to 0.5
- w_out: bfloat16 [128, 128], replicated, may hold values from -0.5 to 0.5
- gain_mid: float32 [128], replicated, may hold values from 0.5 to 2
- chain_len: int32 [4], replicated, may hold values from 1 to 16, 32 in all
- allowed: int32 [4, 4], replicated, may hold values 0 or 1
Outputs:
- update: bfloat16 [512, 512, 128], P('row', 'col')
The draws below stay inside these ranges and needn't reach their ends.
Inputs may be any that keep to these rules, and one draw needn't show every extreme that they name: `chain_len`: chain lengths in blocks of 16 residues; they sum to 32 and the longest is 16.
All inputs are finite; a program needn't handle non-finite values.
Results may differ from the reference program's by a relative error of at most 0.019.
Values may be sent and summed in bfloat16 or wider, within the bound.
A program may use at most 64 MiB of HBM per device.

```python
import math
import jax
import jax.numpy as jnp
import numpy as np
from jax import lax

CZ = 128
CH = 128
BLK = 16
CHAINS = 4
RESIDUES = 512
NBLK = 32
MOST = 16


def place_ends(values, rng, low, high):
    longest = values.shape.index(max(values.shape))
    spots = []
    for shift in (0, 1):
        where = [jax.random.randint(jax.random.fold_in(rng, axis), (), 0, length) for axis, length in enumerate(values.shape)]
        where[longest] = (where[longest] + shift) % values.shape[longest]
        spots.append(tuple(where))
    return values.at[spots[0]].set(low).at[spots[1]].set(high)


def level_of(key, extent, shards, smallest, top_value):
    level, own = 1.0, jax.random.fold_in(key, 6)
    for position, shards_of in shards:
        steps = jnp.exp(jax.random.uniform(jax.random.fold_in(own, position), (shards_of,), jnp.float32, smallest / len(shards), top_value / len(shards)))
        level = level * jnp.repeat(steps, extent[position] // shards_of).reshape([-1 if axis == position else 1 for axis in range(len(extent))])
    return level


def split_up(count, total, limit, slope):
    weights = [(1 << 20) // math.isqrt(grade ** slope) + 1 for grade in range(2, count + 1)]
    spare, counts = total - limit - (count - 1), [1] * (count - 1)
    while spare > 0:
        free = [i for i in range(count - 1) if counts[i] < limit]
        mass, budget = sum([weights[i] for i in free]), spare
        for i in free:
            addition = min(limit - counts[i], max(1, budget * weights[i] // mass), spare)
            counts[i] = counts[i] + addition
            spare = spare - addition
    return np.array([limit] + counts)


def uneven_parts(stream_key, count, total, most, lean):
    if count == 2:
        one = jax.random.randint(stream_key, (), max(1, total - most), min(most, total - 1) + 1)
        return jnp.stack([one, total - one])
    sizes = jnp.asarray(split_up(count, total, most, lean), jnp.int32)
    pairs = (count - 1) // 2
    giver, sink = sizes[1:1 + 2 * pairs:2], sizes[2:2 + 2 * pairs:2]
    room = jnp.minimum(giver - 1, most - sink)
    moved = jax.random.randint(jax.random.fold_in(stream_key, 1), (pairs,), 0, 1 << 20) % (room + 1)
    sizes = sizes.at[1:1 + 2 * pairs:2].set(giver - moved).at[2:2 + 2 * pairs:2].set(sink + moved)
    return sizes[jax.random.permutation(jax.random.fold_in(stream_key, 2), count)]


def bell_draw(rng, dims, spread, reach, pieces=(), held_as=jnp.bfloat16):
    level = level_of(rng, dims, pieces, -0.22, 0.18) if pieces else 1.0
    entries = jax.random.normal(rng, dims, jnp.float32) * spread * level
    return jnp.minimum(jnp.maximum(entries, -reach), reach).astype(held_as)


def setup_inputs(seed: int = 0) -> dict:
    seeds = jax.random.split(jax.random.key(seed), 9)
    return {
        "pair": bell_draw(seeds[0], (RESIDUES, RESIDUES, CZ), 1.0, 6.0, ((0, 32), (1, 16))),
        "gain_in": jnp.clip(jnp.exp(jax.random.uniform(seeds[1], (CZ,), jnp.float32, math.log(0.5), math.log(2.0))), 0.5, 2.0),
        "w_in": bell_draw(seeds[2], (CZ, 4 * CH), CZ ** -0.5, 0.5),
        "w_gate": bell_draw(seeds[3], (CZ, CZ), CZ ** -0.5, 0.5),
        "w_out": bell_draw(seeds[4], (CH, CZ), CH ** -0.5, 0.5),
        "gain_mid": jnp.clip(jnp.exp(jax.random.uniform(seeds[5], (CH,), jnp.float32, math.log(0.5), math.log(2.0))), 0.5, 2.0),
        "chain_len": uneven_parts(seeds[6], CHAINS, NBLK, MOST, 2).astype(jnp.int32),
        "allowed": place_ends((jax.random.randint(seeds[7], (CHAINS, CHAINS), 0, 3) < 2).astype(jnp.int32), jax.random.fold_in(seeds[7], 1), 0, 1),
    }


def layer_norm(values, gain):
    mean = lax.optimization_barrier(jnp.mean(values, axis=-1, keepdims=True))
    centered = values - mean
    var = lax.optimization_barrier(jnp.mean(centered * centered, axis=-1, keepdims=True))
    return centered / jnp.sqrt(var + 1e-05) * gain

def chain_of(positions, chain_len):
    ends = jnp.cumsum(chain_len) * BLK
    return lax.optimization_barrier(jnp.sum((positions[:, None] >= ends[None, :-1]).astype(jnp.int32), axis=1))

def reference(pair, gain_in, w_in, w_gate, w_out, gain_mid, chain_len, allowed):
    positions = jnp.arange(RESIDUES, dtype=jnp.int32)
    chains = chain_of(positions, chain_len)
    hot = (chains[:, None] == jnp.arange(CHAINS, dtype=jnp.int32)[None, :]).astype(jnp.float32)
    mask = jnp.dot(jnp.dot(hot, allowed.astype(jnp.float32)), hot.T)
    normed = layer_norm(pair.astype(jnp.float32), gain_in).astype(jnp.bfloat16)
    flat = normed.reshape(RESIDUES * RESIDUES, CZ)
    proj = jnp.dot(flat, w_in, preferred_element_type=jnp.float32).reshape(RESIDUES, RESIDUES, 4 * CH)
    left = (jax.nn.sigmoid(proj[..., :CH]) * proj[..., CH:2 * CH] * mask[..., None]).astype(jnp.bfloat16)
    right = (jax.nn.sigmoid(proj[..., 2 * CH:3 * CH]) * proj[..., 3 * CH:] * mask[..., None]).astype(jnp.bfloat16)
    mixed = jnp.einsum('ikc,jkc->ijc', left.astype(jnp.float32), right.astype(jnp.float32))
    mixed_norm = layer_norm(mixed, gain_mid).astype(jnp.bfloat16).reshape(RESIDUES * RESIDUES, CH)
    gate = jax.nn.sigmoid(jnp.dot(flat, w_gate, preferred_element_type=jnp.float32))
    out = gate * jnp.dot(mixed_norm, w_out, preferred_element_type=jnp.float32)
    return out.astype(jnp.bfloat16).reshape(RESIDUES, RESIDUES, CZ)
```

```python
import jax
import jax.numpy as jnp
from jax import lax
from jax.experimental import pallas as pl
from jax.experimental.pallas import tpu as pltpu
from jax.sharding import PartitionSpec as P

MESH = pl.DeviceIdType.MESH
F32, BF16 = jnp.float32, jnp.bfloat16
NX, NY, NZ = 4, 8, 8
NG = NY * NZ
EPS = 1e-5


def nt(a, b):
    return lax.dot_general(a, b, (((1,), (1,)), ((), ())), preferred_element_type=F32)


def sigmoid(v):
    return 1.0 / (1.0 + jnp.exp(-v))


def wait_bytes(ref, sem):
    pltpu.make_async_copy(ref, ref, sem).wait()


def kernel(
    pair, gin, win, wgate, wout, gmid, chain_len, allowed, out,
    nb, gate, wt, stage, send, recv, left, right, back, home, final, rows, sems,
):
    row, col = lax.axis_index("row"), lax.axis_index("col")
    z, x = lax.div(row, NX), lax.rem(row, NX)
    y, core = lax.div(col, 2), lax.rem(col, 2)
    me = y * NZ + z

    def plane(n):
        ty = lax.rem(y + lax.div(n, NZ), NY)
        tz = lax.rem(z + lax.rem(n, NZ), NZ)
        return (tz * NX + x, ty * 2 + core), ty * NZ + tz

    beside = (row, col + 1 - 2 * core)
    along = [(z * NX + lax.rem(x + d, NX), col) for d in range(1, NX)]

    barrier = pltpu.get_barrier_semaphore()

    def greet(n, carry):
        pl.semaphore_signal(barrier, inc=1, device_id=plane(n)[0], device_id_type=MESH)
        return carry

    for there in [beside, *along]:
        pl.semaphore_signal(barrier, inc=1, device_id=there, device_id_type=MESH)
    lax.fori_loop(1, NG, greet, 0)

    values = pair[...].reshape(512, 128).astype(F32)
    mean = jnp.mean(values, axis=1, keepdims=True)
    centered = values - mean
    var = jnp.mean(centered * centered, axis=1, keepdims=True)
    normed = (centered * lax.rsqrt(var + EPS) * gin[...]).astype(BF16)
    for i in range(16):
        nb[i % 8, i // 8, core] = normed[i * 32 : (i + 1) * 32]
    for b in range(4):
        wt[b * 128 : (b + 1) * 128, :] = win[:, b * 128 : (b + 1) * 128].astype(F32).T.astype(BF16)

    pl.semaphore_wait(barrier, NG - 1 + NX)
    swap = pltpu.make_async_remote_copy(
        nb.at[:, :, core], nb.at[:, :, core], sems.at[0], sems.at[1], device_id=beside, device_id_type=MESH
    )
    swap.start()

    gate[...] = sigmoid(jnp.dot(normed, wgate[...], preferred_element_type=F32)).reshape(16, 32, 128)

    lane = lax.broadcasted_iota(jnp.int32, (8, 128), 1)
    low = lane < 64
    column = y * 64 + jnp.where(low, lane, lane - 64)
    chain_row, chain_col, end = jnp.int32(0), jnp.zeros((8, 128), jnp.int32), jnp.int32(0)
    for c in range(3):
        end = end + chain_len[c]
        chain_row = chain_row + jnp.where(row >= end, 1, 0)
        chain_col = chain_col + jnp.where(column >= end * 16, 1, 0)
    mask = jnp.zeros((8, 128), F32)
    for b in range(4):
        pick = jnp.int32(0)
        for a in range(4):
            pick = jnp.where(chain_row == a, allowed[a, b], pick)
        mask = jnp.where(chain_col == b, pick.astype(F32), mask)
    mask = mask[0:1]

    half = pl.multiple_of(core * 64, 64)
    weights = jnp.concatenate([wt[pl.ds(b * 128 + half, 64), :] for b in range(4)], axis=0)
    swap.wait()
    for t in range(8):
        proj = nt(weights, nb[t].reshape(128, 128))
        stage[pl.ds(t, 64, stride=16), :] = sigmoid(proj[:64]) * proj[64:128] * mask
        stage[pl.ds(8 + t, 64, stride=16), :] = sigmoid(proj[128:192]) * proj[192:] * mask
    send[...] = stage[...].reshape(64, 16, 128).astype(BF16)

    def give(n, carry):
        there, index = plane(n)
        pltpu.make_async_remote_copy(
            send.at[index], recv.at[me], sems.at[2], sems.at[3], device_id=there, device_id_type=MESH
        ).start()
        return carry

    lax.fori_loop(1, NG, give, 0)
    pltpu.make_async_copy(send.at[me], recv.at[me], sems.at[3]).start()
    wait_bytes(recv, sems.at[3])

    wide = lax.broadcasted_iota(jnp.int32, (16, 128), 1) < 64
    for zz in range(8):
        for q in range(4):
            one = recv[(2 * q) * NZ + zz].astype(F32)
            two = recv[(2 * q + 1) * NZ + zz].astype(F32)
            first = jnp.where(wide, one, pltpu.roll(two, 64, 1))
            second = jnp.where(wide, pltpu.roll(one, 64, 1), two)
            at = slice(q * 128, (q + 1) * 128)
            left[zz, :, at] = jnp.concatenate([first[:8], second[:8]], axis=0).astype(BF16)
            right[zz, x, :, at] = jnp.concatenate([first[8:], second[8:]], axis=0).astype(BF16)

    for there in along:
        pltpu.make_async_remote_copy(
            right.at[:, x], right.at[:, x], sems.at[4], sems.at[5], device_id=there, device_id_type=MESH
        ).start()
    wait_bytes(right.at[:, pl.ds(0, NX - 1)], sems.at[5])

    lhs = left[...].reshape(128, 512)
    for p in range(4):
        sums = nt(lhs, right[2 * p : 2 * p + 2].reshape(128, 512))
        for zz in range(8):
            one, two = sums[zz * 16 : zz * 16 + 8], sums[zz * 16 + 8 : zz * 16 + 16]
            back[2 * p * NZ + zz] = jnp.where(low, one, pltpu.roll(two, 64, 1)).astype(BF16)
            back[(2 * p + 1) * NZ + zz] = jnp.where(low, pltpu.roll(one, 64, 1), two).astype(BF16)

    def give_back(n, carry):
        there, index = plane(n)
        pltpu.make_async_remote_copy(
            back.at[index], home.at[core, me], sems.at[6], sems.at[7], device_id=there, device_id_type=MESH
        ).start()
        return carry

    lax.fori_loop(1, NG, give_back, 0)
    pltpu.make_async_copy(back.at[me], home.at[core, me], sems.at[7]).start()
    wait_bytes(home.at[core], sems.at[7])
    swap2 = pltpu.make_async_remote_copy(
        home.at[core], home.at[core], sems.at[8], sems.at[9], device_id=beside, device_id_type=MESH
    )
    swap2.start()
    gain = jnp.broadcast_to(gmid[...], (128, 128)).T
    swap2.wait()

    final[...] = home[...].reshape(1024, 128).astype(F32)
    for t in range(8):
        mixed = final[pl.ds(t, 128, stride=8), :]
        mean = jnp.mean(mixed, axis=0, keepdims=True)
        centered = mixed - mean
        var = jnp.mean(centered * centered, axis=0, keepdims=True)
        mixed_norm = (centered * lax.rsqrt(var + EPS) * gain).astype(BF16)
        rows[t] = lax.dot_general(
            mixed_norm, wout[...], (((0,), (0,)), ((), ())), preferred_element_type=F32
        )
        for h in range(2):
            own = pl.multiple_of(h * 64 + core * 32, 32)
            out[8 * h + t] = (gate[8 * h + t] * rows[t, pl.ds(own, 32), :]).astype(BF16)

    wait_bytes(send.at[pl.ds(0, NG - 1)], sems.at[2])
    wait_bytes(right.at[:, pl.ds(0, NX - 1)], sems.at[4])
    wait_bytes(back.at[pl.ds(0, NG - 1)], sems.at[6])


def on_device(pair, gain_in, w_in, w_gate, w_out, gain_mid, chain_len, allowed):
    vmem, smem = pl.BlockSpec(memory_space=pltpu.VMEM), pl.BlockSpec(memory_space=pltpu.SMEM)
    return pl.pallas_call(
        kernel,
        out_shape=jax.ShapeDtypeStruct(pair.shape, pair.dtype),
        in_specs=[vmem] * 6 + [smem] * 2,
        out_specs=vmem,
        scratch_shapes=[
            pltpu.VMEM((8, 2, 2, 32, 128), BF16),
            pltpu.VMEM((16, 32, 128), F32),
            pltpu.VMEM((512, 128), BF16),
            pltpu.VMEM((1024, 128), F32),
            pltpu.VMEM((NG, 16, 128), BF16),
            pltpu.VMEM((NG, 16, 128), BF16),
            pltpu.VMEM((8, 16, 512), BF16),
            pltpu.VMEM((8, NX, 16, 512), BF16),
            pltpu.VMEM((NG, 8, 128), BF16),
            pltpu.VMEM((2, NG, 8, 128), BF16),
            pltpu.VMEM((1024, 128), F32),
            pltpu.VMEM((8, 128, 128), F32),
            pltpu.SemaphoreType.DMA((10,)),
        ],
        compiler_params=pltpu.CompilerParams(
            collective_id=0, has_side_effects=True, vmem_limit_bytes=32 * 2**20
        ),
    )(pair, gain_in.reshape(1, 128), w_in, w_gate, w_out, gain_mid.reshape(1, 128), chain_len, allowed)


def solution(mesh):
    return jax.shard_map(
        on_device,
        mesh=mesh,
        in_specs=(P("row", "col", None), P(), P(), P(), P(), P(), P(), P()),
        out_specs=P("row", "col", None),
        check_vma=False,
    )
```

```python
import jax
import jax.numpy as jnp
from jax import lax
from jax.experimental import pallas as pl
from jax.experimental.pallas import tpu as pltpu
from jax.sharding import PartitionSpec as P

MESH = pl.DeviceIdType.MESH
F32, BF16 = jnp.float32, jnp.bfloat16
NX, NY, NZ = 4, 8, 8
NG = NY * NZ
ORDER = (2, 1, 3, 0)
EPS = 1e-5
SWAP, LEFT, GATHER, BACK, SWAP2, SENT, LOAD = 0, 2, 3, 16, 17, 19, 24


def nt(a, b):
    return lax.dot_general(a, b, (((1,), (1,)), ((), ())), preferred_element_type=F32)


def sigmoid(v):
    return 1.0 / (1.0 + jnp.exp(-v))


def wait_bytes(ref, sem):
    pltpu.make_async_copy(ref, ref, sem).wait()


def kernel(
    pair_hbm, gin_hbm, win_hbm, wgate_hbm, wout_hbm, gmid_hbm, len_hbm, allowed_hbm, out,
    pair, gin, win, wgate, wout, gmid, chain_len, allowed,
    nb, gate, wt, stage, send_r, send_l, recv_r, recv_l, left, right, back, home, final, rows, sems, arrive,
):
    row, col = lax.axis_index("row"), lax.axis_index("col")
    z, x = lax.div(row, NX), lax.rem(row, NX)
    y, core = lax.div(col, 2), lax.rem(col, 2)
    zp, zb = lax.div(z, 2), lax.rem(z, 2)
    me = y * NZ + z

    def chip(ty, tz):
        return (tz * NX + x, ty * 2 + core)

    def plane(n):
        ty = lax.rem(y + lax.div(n, NZ), NY)
        tz = lax.rem(z + lax.rem(n, NZ), NZ)
        return chip(ty, tz), ty * NZ + tz

    def remote(src, dst, sent, arrived, there):
        return pltpu.make_async_remote_copy(src, dst, sent, arrived, device_id=there, device_id_type=MESH)

    beside = (row, col + 1 - 2 * core)
    x_up, x_down = lax.rem(x + 1, NX), lax.rem(x + NX - 1, NX)
    up, down = (z * NX + x_up, col), (z * NX + x_down, col)

    loads = [
        pltpu.make_async_copy(src, dst, sems.at[LOAD + n])
        for n, (src, dst) in enumerate(
            [(pair_hbm, pair), (gin_hbm, gin), (win_hbm, win), (wgate_hbm, wgate), (wout_hbm, wout),
             (gmid_hbm, gmid), (len_hbm, chain_len), (allowed_hbm, allowed)]
        )
    ]
    for load in loads:
        load.start()

    barrier = pltpu.get_barrier_semaphore()

    def greet(n, carry):
        pl.semaphore_signal(barrier, inc=1, device_id=plane(n)[0], device_id_type=MESH)
        return carry

    lax.fori_loop(1, NG, greet, 0)
    for there in (beside, up, down):
        pl.semaphore_signal(barrier, inc=1, device_id=there, device_id_type=MESH)

    loads[0].wait()
    loads[1].wait()
    values = pair[...].reshape(512, 128).astype(F32)
    mean = jnp.mean(values, axis=1, keepdims=True)
    centered = values - mean
    var = jnp.mean(centered * centered, axis=1, keepdims=True)
    normed = (centered * lax.rsqrt(var + EPS) * gin[...]).astype(BF16)
    for i in range(16):
        nb[i % 8, i // 8, core] = normed[i * 32 : (i + 1) * 32]
    loads[2].wait()
    for b in range(4):
        wt[b * 128 : (b + 1) * 128, :] = win[:, b * 128 : (b + 1) * 128].astype(F32).T.astype(BF16)
    for load in loads[3:]:
        load.wait()

    pl.semaphore_wait(barrier, NG + 2)
    swap = remote(nb.at[:, :, core], nb.at[:, :, core], sems.at[SWAP], sems.at[SWAP + 1], beside)
    swap.start()

    gate[...] = sigmoid(jnp.dot(normed, wgate[...], preferred_element_type=F32)).reshape(16, 32, 128)

    lane = lax.broadcasted_iota(jnp.int32, (8, 128), 1)
    low = lane < 64
    column = y * 64 + jnp.where(low, lane, lane - 64)
    chain_row, chain_col, end = jnp.int32(0), jnp.zeros((8, 128), jnp.int32), jnp.int32(0)
    for c in range(3):
        end = end + chain_len[c]
        chain_row = chain_row + jnp.where(row >= end, 1, 0)
        chain_col = chain_col + jnp.where(column >= end * 16, 1, 0)
    mask = jnp.zeros((8, 128), F32)
    for b in range(4):
        pick = jnp.int32(0)
        for a in range(4):
            pick = jnp.where(chain_row == a, allowed[a, b], pick)
        mask = jnp.where(chain_col == b, pick.astype(F32), mask)
    mask = mask[0:1]

    half = pl.multiple_of(core * 64, 64)

    def project(first, store):
        weights = jnp.concatenate(
            [wt[pl.ds(b * 128 + half, 64), :] for b in (first, first + 1)], axis=0
        )
        for t in range(8):
            proj = nt(weights, nb[t].reshape(128, 128))
            stage[pl.ds(t, 64, stride=8), :] = sigmoid(proj[:64]) * proj[64:] * mask
        store[...] = stage[...].reshape(64, 8, 128).astype(BF16)

    swap.wait()
    project(2, send_r)
    for r in ORDER:
        tp = lax.rem(zp + 4 - r, 4)
        for b in range(2):
            tz = tp * 2 + b

            def give(dy, carry, tz=tz, r=r):
                ty = lax.rem(y + dy, NY)
                remote(
                    send_r.at[ty * NZ + tz], recv_r.at[zp, zb, y], sems.at[SENT], arrive.at[r], chip(ty, tz)
                ).start()
                return carry

            lax.fori_loop(1, NY, give, 0)
            if r:
                give(0, 0)
            else:

                @pl.when(tz != z)
                def _(give=give):
                    give(0, 0)

    pltpu.make_async_copy(send_r.at[me], recv_r.at[zp, zb, y], arrive.at[0]).start()

    project(0, send_l)

    def give_left(n, carry):
        there, index = plane(n)
        remote(send_l.at[index], recv_l.at[z, y], sems.at[SENT + 1], sems.at[LEFT], there).start()
        return carry

    lax.fori_loop(1, NG, give_left, 0)
    pltpu.make_async_copy(send_l.at[me], recv_l.at[z, y], sems.at[LEFT]).start()

    def merge(one, two):
        one, two = one.astype(F32), two.astype(F32)
        first = jnp.where(low, one, pltpu.roll(two, 64, 1))
        second = jnp.where(low, pltpu.roll(one, 64, 1), two)
        return jnp.concatenate([first, second], axis=0).astype(BF16)

    def own(p):
        return right.at[p, :, x]

    for r in ORDER:
        p = lax.rem(zp + r, 4)
        wait_bytes(recv_r.at[p], arrive.at[r])
        for b in range(2):
            for q in range(4):
                right[p, b, x, :, q * 128 : (q + 1) * 128] = merge(recv_r[p, b, 2 * q], recv_r[p, b, 2 * q + 1])
        remote(own(p), own(p), sems.at[SENT + 2], sems.at[GATHER + r], up).start()
        remote(own(p), own(p), sems.at[SENT + 2], sems.at[GATHER + 4 + r], down).start()

    for n, r in enumerate(ORDER):
        p = lax.rem(zp + r, 4)
        came, there, source = ((GATHER, up, x_down), (GATHER + 4, down, x_up))[n % 2]
        wait_bytes(right.at[p, :, source], sems.at[came + r])
        remote(
            right.at[p, :, source], right.at[p, :, source], sems.at[SENT + 2], sems.at[GATHER + 8 + r], there
        ).start()

    wait_bytes(recv_l, sems.at[LEFT])
    for zz in range(8):
        for q in range(4):
            left[zz, :, q * 128 : (q + 1) * 128] = merge(recv_l[zz, 2 * q], recv_l[zz, 2 * q + 1])

    lhs = left[...].reshape(128, 512)
    x_far = lax.rem(x + 2, NX)
    for n, r in enumerate(ORDER):
        p = lax.rem(zp + r, 4)
        came, source = ((GATHER + 4, x_up), (GATHER, x_down))[n % 2]
        wait_bytes(right.at[p, :, source], sems.at[came + r])
        wait_bytes(right.at[p, :, x_far], sems.at[GATHER + 8 + r])
        sums = nt(lhs, right[p].reshape(128, 512))
        for zz in range(8):
            one, two = sums[zz * 16 : zz * 16 + 8], sums[zz * 16 + 8 : zz * 16 + 16]
            back[p, 0, zz] = jnp.where(low, one, pltpu.roll(two, 64, 1)).astype(BF16)
            back[p, 1, zz] = jnp.where(low, pltpu.roll(one, 64, 1), two).astype(BF16)
        for b in range(2):
            ty = p * 2 + b

            def give_back(dz, carry, ty=ty, p=p, b=b):
                tz = lax.rem(z + dz, NZ)
                remote(back.at[p, b, tz], home.at[core, me], sems.at[SENT + 3], sems.at[BACK], chip(ty, tz)).start()
                return carry

            lax.fori_loop(1, NZ, give_back, 0)

            @pl.when(ty != y)
            def _(give_back=give_back):
                give_back(0, 0)

    pltpu.make_async_copy(back.at[lax.div(y, 2), lax.rem(y, 2), z], home.at[core, me], sems.at[BACK]).start()
    gain = jnp.broadcast_to(gmid[...], (128, 128)).T
    wait_bytes(home.at[core], sems.at[BACK])
    swap2 = remote(home.at[core], home.at[core], sems.at[SWAP2], sems.at[SWAP2 + 1], beside)
    swap2.start()
    swap2.wait()

    final[...] = home[...].reshape(1024, 128).astype(F32)
    for t in range(8):
        mixed = final[pl.ds(t, 128, stride=8), :]
        mean = jnp.mean(mixed, axis=0, keepdims=True)
        centered = mixed - mean
        var = jnp.mean(centered * centered, axis=0, keepdims=True)
        mixed_norm = (centered * lax.rsqrt(var + EPS) * gain).astype(BF16)
        rows[t] = lax.dot_general(
            mixed_norm, wout[...], (((0,), (0,)), ((), ())), preferred_element_type=F32
        )
        for h in range(2):
            mine = pl.multiple_of(h * 64 + core * 32, 32)
            out[8 * h + t] = (gate[8 * h + t] * rows[t, pl.ds(mine, 32), :]).astype(BF16)

    wait_bytes(send_r.at[pl.ds(0, NG - 1)], sems.at[SENT])
    wait_bytes(send_l.at[pl.ds(0, NG - 1)], sems.at[SENT + 1])
    wait_bytes(right.at[:, :, pl.ds(0, 3)], sems.at[SENT + 2])
    wait_bytes(send_l.at[pl.ds(0, NG - 1)], sems.at[SENT + 3])


def on_device(pair, gain_in, w_in, w_gate, w_out, gain_mid, chain_len, allowed):
    operands = (pair, gain_in.reshape(1, 128), w_in, w_gate, w_out, gain_mid.reshape(1, 128))
    scalars = (chain_len, allowed)
    return pl.pallas_call(
        kernel,
        out_shape=jax.ShapeDtypeStruct(pair.shape, pair.dtype),
        in_specs=[pl.BlockSpec(memory_space=pl.ANY)] * 8,
        out_specs=pl.BlockSpec(memory_space=pltpu.VMEM),
        scratch_shapes=[
            *[pltpu.VMEM(a.shape, a.dtype) for a in operands],
            *[pltpu.SMEM(a.shape, a.dtype) for a in scalars],
            pltpu.VMEM((8, 2, 2, 32, 128), BF16),
            pltpu.VMEM((16, 32, 128), F32),
            pltpu.VMEM((512, 128), BF16),
            pltpu.VMEM((512, 128), F32),
            pltpu.VMEM((NG, 8, 128), BF16),
            pltpu.VMEM((NG, 8, 128), BF16),
            pltpu.VMEM((4, 2, NY, 8, 128), BF16),
            pltpu.VMEM((NZ, NY, 8, 128), BF16),
            pltpu.VMEM((NZ, 16, 512), BF16),
            pltpu.VMEM((4, 2, NX, 16, 512), BF16),
            pltpu.VMEM((4, 2, NZ, 8, 128), BF16),
            pltpu.VMEM((2, NG, 8, 128), BF16),
            pltpu.VMEM((1024, 128), F32),
            pltpu.VMEM((8, 128, 128), F32),
            pltpu.SemaphoreType.DMA((32,)),
            pltpu.SemaphoreType.DMA((4,)),
        ],
        compiler_params=pltpu.CompilerParams(
            collective_id=0, has_side_effects=True, vmem_limit_bytes=56 * 2**20
        ),
    )(*operands, *scalars)


def solution(mesh):
    return jax.shard_map(
        on_device,
        mesh=mesh,
        in_specs=(P("row", "col", None), P(), P(), P(), P(), P(), P(), P()),
        out_specs=P("row", "col", None),
        check_vma=False,
    )
```

```python
import jax
import jax.numpy as jnp
from jax import lax
from jax.experimental import pallas as pl
from jax.experimental.pallas import tpu as pltpu
from jax.sharding import PartitionSpec as P

MESH = pl.DeviceIdType.MESH
F32, BF16 = jnp.float32, jnp.bfloat16
NX, NY, NZ = 4, 8, 8
NG = NY * NZ
ORDER = (0, 1, 3, 2)
EPS = 1e-5
SWAP, LEFT, GATHER, BACK, SWAP2, SENT, LOAD = 0, 2, 3, 15, 19, 21, 25


def nt(a, b):
    return lax.dot_general(a, b, (((1,), (1,)), ((), ())), preferred_element_type=F32)


def sigmoid(v):
    return 1.0 / (1.0 + jnp.exp(-v))


def wait_bytes(ref, sem):
    pltpu.make_async_copy(ref, ref, sem).wait()


def kernel(
    pair_hbm, gin_hbm, win_hbm, wgate_hbm, wout_hbm, gmid_hbm, len_hbm, allowed_hbm, out,
    pair, gin, win, wgate, wout, gmid, chain_len, allowed,
    nb, gate, wt, stage, send_r, send_l, recv_r, recv_l, left, right, back, home, final, rows, sems, arrive,
):
    row, col = lax.axis_index("row"), lax.axis_index("col")
    z, x = lax.div(row, NX), lax.rem(row, NX)
    y, core = lax.div(col, 2), lax.rem(col, 2)
    zp, zb = lax.div(z, 2), lax.rem(z, 2)
    me = z * NY + y

    def chip(ty, tz):
        return (tz * NX + x, ty * 2 + core)

    def plane(n):
        ty = lax.rem(y + lax.div(n, NZ), NY)
        tz = lax.rem(z + lax.rem(n, NZ), NZ)
        return chip(ty, tz)

    def remote(src, dst, sent, arrived, there):
        return pltpu.make_async_remote_copy(src, dst, sent, arrived, device_id=there, device_id_type=MESH)

    beside = (row, col + 1 - 2 * core)
    x_up, x_down = lax.rem(x + 1, NX), lax.rem(x + NX - 1, NX)
    up, down, far = (z * NX + x_up, col), (z * NX + x_down, col), (z * NX + lax.rem(x + 2, NX), col)

    loads = [
        pltpu.make_async_copy(src, dst, sems.at[LOAD + n])
        for n, (src, dst) in enumerate(
            [(pair_hbm, pair), (gin_hbm, gin), (win_hbm, win), (wgate_hbm, wgate), (wout_hbm, wout),
             (gmid_hbm, gmid), (len_hbm, chain_len), (allowed_hbm, allowed)]
        )
    ]
    for load in loads:
        load.start()

    barrier = pltpu.get_barrier_semaphore()

    for n in range(1, NG):
        pl.semaphore_signal(barrier, inc=1, device_id=plane(n), device_id_type=MESH)
    for there in (beside, up, down, far):
        pl.semaphore_signal(barrier, inc=1, device_id=there, device_id_type=MESH)

    loads[0].wait()
    loads[1].wait()
    values = pair[...].reshape(512, 128).astype(F32)
    mean = jnp.mean(values, axis=1, keepdims=True)
    centered = values - mean
    var = jnp.mean(centered * centered, axis=1, keepdims=True)
    normed = (centered * lax.rsqrt(var + EPS) * gin[...]).astype(BF16)
    for i in range(16):
        nb[i % 8, i // 8, core] = normed[i * 32 : (i + 1) * 32]
    loads[2].wait()
    for b in range(4):
        wt[b * 128 : (b + 1) * 128, :] = win[:, b * 128 : (b + 1) * 128].astype(F32).T.astype(BF16)
    for load in loads[3:]:
        load.wait()

    pl.semaphore_wait(barrier, NG + 3)
    swap = remote(nb.at[:, :, core], nb.at[:, :, core], sems.at[SWAP], sems.at[SWAP + 1], beside)
    swap.start()

    gate[...] = sigmoid(jnp.dot(normed, wgate[...], preferred_element_type=F32)).reshape(16, 32, 128)

    lane = lax.broadcasted_iota(jnp.int32, (8, 128), 1)
    low = lane < 64
    column = y * 64 + jnp.where(low, lane, lane - 64)
    chain_row, chain_col, end = jnp.int32(0), jnp.zeros((8, 128), jnp.int32), jnp.int32(0)
    for c in range(3):
        end = end + chain_len[c]
        chain_row = chain_row + jnp.where(row >= end, 1, 0)
        chain_col = chain_col + jnp.where(column >= end * 16, 1, 0)
    mask = jnp.zeros((8, 128), F32)
    for b in range(4):
        pick = jnp.int32(0)
        for a in range(4):
            pick = jnp.where(chain_row == a, allowed[a, b], pick)
        mask = jnp.where(chain_col == b, pick.astype(F32), mask)
    mask = mask[0:1]

    half = pl.multiple_of(core * 64, 64)

    def project(first, store):
        weights = jnp.concatenate(
            [wt[pl.ds(b * 128 + half, 64), :] for b in (first, first + 1)], axis=0
        )
        for t in range(8):
            proj = nt(weights, nb[t].reshape(128, 128))
            stage[pl.ds(t, 64, stride=8), :] = sigmoid(proj[:64]) * proj[64:] * mask
        store[...] = stage[...].reshape(64, 8, 128).astype(BF16)

    swap.wait()
    project(2, send_r)
    others = [(dy, dz) for dz in reversed(range(NZ)) for dy in range(NY) if dy or dz]

    for dy, dz in others:
        ty, tz = lax.rem(y + dy, NY), lax.rem(z + dz, NZ)
        remote(
            send_r.at[tz * NY + ty], recv_r.at[zp, zb, y], sems.at[SENT], arrive.at[zp], chip(ty, tz)
        ).start()
    pltpu.make_async_copy(send_r.at[me], recv_r.at[zp, zb, y], arrive.at[zp]).start()

    project(0, send_l)

    for dy, dz in others:
        ty, tz = lax.rem(y + dy, NY), lax.rem(z + dz, NZ)
        remote(send_l.at[tz * NY + ty], recv_l.at[z, y], sems.at[SENT + 1], sems.at[LEFT], chip(ty, tz)).start()

    pltpu.make_async_copy(send_l.at[me], recv_l.at[z, y], sems.at[LEFT]).start()

    def merge(one, two):
        one, two = one.astype(F32), two.astype(F32)
        first = jnp.where(low, one, pltpu.roll(two, 64, 1))
        second = jnp.where(low, pltpu.roll(one, 64, 1), two)
        return jnp.concatenate([first, second], axis=0).astype(BF16)

    def own(p):
        return right.at[p, :, x]

    x_far = lax.rem(x + 2, NX)
    routes = [((GATHER, up, x_down), (GATHER + 4, x_up)), ((GATHER + 4, down, x_up), (GATHER, x_down))] * 2

    def spread(p):
        wait_bytes(recv_r.at[p], arrive.at[p])
        for b in range(2):
            for q in range(4):
                right[p, b, x, :, q * 128 : (q + 1) * 128] = merge(recv_r[p, b, 2 * q], recv_r[p, b, 2 * q + 1])
        remote(own(p), own(p), sems.at[SENT + 2], sems.at[GATHER + p], up).start()
        remote(own(p), own(p), sems.at[SENT + 2], sems.at[GATHER + 4 + p], down).start()
        remote(own(p), own(p), sems.at[SENT + 2], sems.at[GATHER + 8 + p], far).start()

    def contract(p):
        wait_bytes(right.at[p, :, x_down], sems.at[GATHER + p])
        wait_bytes(right.at[p, :, x_up], sems.at[GATHER + 4 + p])
        wait_bytes(right.at[p, :, x_far], sems.at[GATHER + 8 + p])
        sums = nt(left[...].reshape(128, 512), right[p].reshape(128, 512))
        for zz in range(8):
            one, two = sums[zz * 16 : zz * 16 + 8], sums[zz * 16 + 8 : zz * 16 + 16]
            back[p, 0, zz] = jnp.where(low, one, pltpu.roll(two, 64, 1)).astype(BF16)
            back[p, 1, zz] = jnp.where(low, pltpu.roll(one, 64, 1), two).astype(BF16)
        def give_back(b, tz):
            remote(
                back.at[p, b, tz], home.at[core, me], sems.at[SENT + 3], sems.at[BACK + zp], chip(p * 2 + b, tz)
            ).start()

        for dz in range(1, NZ):
            for b in range(2):
                give_back(b, lax.rem(z + dz, NZ))
        for b in range(2):

            @pl.when(p * 2 + b != y)
            def _(b=b):
                give_back(b, z)

    c0, c1, c2, c3 = ORDER
    spread(c0)
    spread(c1)
    spread(c2)
    spread(c3)
    wait_bytes(recv_l, sems.at[LEFT])
    for zz in range(8):
        for q in range(4):
            left[zz, :, q * 128 : (q + 1) * 128] = merge(recv_l[zz, 2 * q], recv_l[zz, 2 * q + 1])
    contract(c0)
    contract(c1)
    contract(c2)
    contract(c3)
    pltpu.make_async_copy(back.at[lax.div(y, 2), lax.rem(y, 2), z], home.at[core, me], sems.at[BACK + zp]).start()
    gain = jnp.broadcast_to(gmid[...], (128, 128)).T
    for q in range(4):
        part = home.at[core, pl.ds(q * 16, 16)]
        wait_bytes(part, sems.at[BACK + q])
        remote(part, part, sems.at[SWAP2], sems.at[SWAP2 + 1], beside).start()
    wait_bytes(home.at[core], sems.at[SWAP2 + 1])

    final[...] = home[...].reshape(1024, 128).astype(F32)
    for t in range(8):
        mixed = final[pl.ds(t, 128, stride=8), :]
        mean = jnp.mean(mixed, axis=0, keepdims=True)
        centered = mixed - mean
        var = jnp.mean(centered * centered, axis=0, keepdims=True)
        mixed_norm = (centered * lax.rsqrt(var + EPS) * gain).astype(BF16)
        rows[t] = lax.dot_general(
            mixed_norm, wout[...], (((0,), (0,)), ((), ())), preferred_element_type=F32
        )
        for h in range(2):
            mine = pl.multiple_of(h * 64 + core * 32, 32)
            out[8 * h + t] = (gate[8 * h + t] * rows[t, pl.ds(mine, 32), :]).astype(BF16)

    wait_bytes(send_r.at[pl.ds(0, NG - 1)], sems.at[SENT])
    wait_bytes(send_l.at[pl.ds(0, NG - 1)], sems.at[SENT + 1])
    wait_bytes(right.at[:, :, pl.ds(0, 3)], sems.at[SENT + 2])
    wait_bytes(send_l.at[pl.ds(0, NG - 1)], sems.at[SENT + 3])
    wait_bytes(home.at[core], sems.at[SWAP2])


def on_device(pair, gain_in, w_in, w_gate, w_out, gain_mid, chain_len, allowed):
    operands = (pair, gain_in.reshape(1, 128), w_in, w_gate, w_out, gain_mid.reshape(1, 128))
    scalars = (chain_len, allowed)
    return pl.pallas_call(
        kernel,
        out_shape=jax.ShapeDtypeStruct(pair.shape, pair.dtype),
        in_specs=[pl.BlockSpec(memory_space=pl.ANY)] * 8,
        out_specs=pl.BlockSpec(memory_space=pltpu.VMEM),
        scratch_shapes=[
            *[pltpu.VMEM(a.shape, a.dtype) for a in operands],
            *[pltpu.SMEM(a.shape, a.dtype) for a in scalars],
            pltpu.VMEM((8, 2, 2, 32, 128), BF16),
            pltpu.VMEM((16, 32, 128), F32),
            pltpu.VMEM((512, 128), BF16),
            pltpu.VMEM((512, 128), F32),
            pltpu.VMEM((NG, 8, 128), BF16),
            pltpu.VMEM((NG, 8, 128), BF16),
            pltpu.VMEM((4, 2, NY, 8, 128), BF16),
            pltpu.VMEM((NZ, NY, 8, 128), BF16),
            pltpu.VMEM((NZ, 16, 512), BF16),
            pltpu.VMEM((4, 2, NX, 16, 512), BF16),
            pltpu.VMEM((4, 2, NZ, 8, 128), BF16),
            pltpu.VMEM((2, NG, 8, 128), BF16),
            pltpu.VMEM((1024, 128), F32),
            pltpu.VMEM((8, 128, 128), F32),
            pltpu.SemaphoreType.DMA((33,)),
            pltpu.SemaphoreType.DMA((4,)),
        ],
        compiler_params=pltpu.CompilerParams(
            collective_id=0, has_side_effects=True, vmem_limit_bytes=32 * 2**20
        ),
    )(*[pltpu.with_memory_space_constraint(a, pltpu.HBM) for a in (*operands, *scalars)])


def solution(mesh):
    return jax.shard_map(
        on_device,
        mesh=mesh,
        in_specs=(P("row", "col", None), P(), P(), P(), P(), P(), P(), P()),
        out_specs=P("row", "col", None),
        check_vma=False,
    )
```

```python
import jax
import jax.numpy as jnp
from jax import lax
from jax.experimental import pallas as pl
from jax.experimental.pallas import tpu as pltpu
from jax.sharding import PartitionSpec as P

MESH = pl.DeviceIdType.MESH
F32, BF16 = jnp.float32, jnp.bfloat16
NX, NY, NZ = 4, 8, 8
NG = NY * NZ
ORDER = (0, 1, 3, 2)
EPS = 1e-5
RIGHT, LEFT, GATHER, ADD, BACK, SENT, LOAD = 0, 4, 5, 17, 21, 22, 27


def nt(a, b):
    return lax.dot_general(a, b, (((1,), (1,)), ((), ())), preferred_element_type=F32)


def sigmoid(v):
    return 1.0 / (1.0 + jnp.exp(-v))


def wait_bytes(ref, sem):
    pltpu.make_async_copy(ref, ref, sem).wait()


def kernel(
    pair_hbm, gin_hbm, win_hbm, wgate_hbm, wout_hbm, gmid_hbm, len_hbm, allowed_hbm, out,
    pair, gin, win, wgate, wout, gmid, chain_len, allowed,
    gate, wt, stage, send_r, send_l, recv_r, recv_l, left, right, part, other, back, home, final, sems,
):
    row, col = lax.axis_index("row"), lax.axis_index("col")
    z, x = lax.div(row, NX), lax.rem(row, NX)
    y, core = lax.div(col, 2), lax.rem(col, 2)
    zp, zb = lax.div(z, 2), lax.rem(z, 2)
    xh, xl = lax.div(x, 2), lax.rem(x, 2)
    me = z * NY + y

    def chip(ty, tz):
        return (tz * NX + x, ty * 2 + core)

    def remote(src, dst, sent, arrived, there):
        return pltpu.make_async_remote_copy(
            src, dst, sems.at[sent], sems.at[arrived], device_id=there, device_id_type=MESH
        )

    beside = (row, col + 1 - 2 * core)
    along = [(d, (z * NX + lax.rem(x + d, NX), col)) for d in (2, 1, 3)]

    loads = [
        pltpu.make_async_copy(src, dst, sems.at[LOAD + n])
        for n, (src, dst) in enumerate(
            [(pair_hbm, pair), (gin_hbm, gin), (win_hbm, win), (wgate_hbm, wgate), (wout_hbm, wout),
             (gmid_hbm, gmid), (len_hbm, chain_len), (allowed_hbm, allowed)]
        )
    ]
    for load in loads:
        load.start()

    ring = [(dy, dz) for dy in range(NY) for dz in range(NZ) if dy or dz]
    ring.sort(key=lambda o: -min(o[0], NY - o[0]) - min(o[1], NZ - o[1]))
    barrier = pltpu.get_barrier_semaphore()
    for dy, dz in ring:
        there = chip(lax.rem(y + dy, NY), lax.rem(z + dz, NZ))
        pl.semaphore_signal(barrier, inc=1, device_id=there, device_id_type=MESH)
    for there in [beside] + [there for _, there in along]:
        pl.semaphore_signal(barrier, inc=1, device_id=there, device_id_type=MESH)

    lane = lax.broadcasted_iota(jnp.int32, (8, 128), 1)
    low = lane < 64
    lane32 = jnp.where(low, lane, lane - 64)
    even = lane32 < 32
    lane32 = jnp.where(even, lane32, lane32 - 32)

    def half_roll(v):
        return pltpu.roll(v, 64, 1)

    loads[0].wait()
    loads[1].wait()
    values = pair[...].reshape(512, 128).astype(F32)
    mean = jnp.mean(values, axis=1, keepdims=True)
    centered = values - mean
    var = jnp.mean(centered * centered, axis=1, keepdims=True)
    normed = (centered * lax.rsqrt(var + EPS) * gin[...]).astype(BF16)
    loads[2].wait()
    for b in range(4):
        wt[b * 128 : (b + 1) * 128, :] = win[:, b * 128 : (b + 1) * 128].astype(F32).T.astype(BF16)
    for load in loads[3:]:
        load.wait()

    column = col * 32 + lane32
    chain_row, chain_col, end = jnp.int32(0), jnp.zeros((8, 128), jnp.int32), jnp.int32(0)
    for c in range(3):
        end = end + chain_len[c]
        chain_row = chain_row + jnp.where(row >= end, 1, 0)
        chain_col = chain_col + jnp.where(column >= end * 16, 1, 0)
    mask = jnp.zeros((8, 128), F32)
    for b in range(4):
        pick = jnp.int32(0)
        for a in range(4):
            pick = jnp.where(chain_row == a, allowed[a, b], pick)
        mask = jnp.where(chain_col == b, pick.astype(F32), mask)
    mask = mask[0:1]

    wide_low = lax.broadcasted_iota(jnp.int32, (64, 128), 1) < 64

    def project(first, store):
        weights = wt[first * 128 : (first + 2) * 128, :]
        for t in range(0, 8, 2):
            four = [normed[i * 32 : (i + 1) * 32] for i in (t, 8 + t, t + 1, 9 + t)]
            proj = nt(weights, jnp.concatenate(four, axis=0))
            gated = sigmoid(proj[:128]) * proj[128:] * mask
            one, two = gated[:64], gated[64:]
            stage[pl.ds(t, 64, stride=8), :] = jnp.where(wide_low, one, half_roll(two))
            stage[pl.ds(t + 1, 64, stride=8), :] = jnp.where(wide_low, half_roll(one), two)
        store[...] = stage[...].reshape(64, 8, 128).astype(BF16)

    project(2, send_r)
    project(0, send_l)
    gate[...] = sigmoid(jnp.dot(normed, wgate[...], preferred_element_type=F32)).reshape(16, 32, 128)
    gain = jnp.broadcast_to(gmid[...], (128, 128)).T

    pl.semaphore_wait(barrier, NG + 3)
    for dy, dz in ring:
        ty, tz = lax.rem(y + dy, NY), lax.rem(z + dz, NZ)
        remote(send_r.at[tz * NY + ty], recv_r.at[zp, zb, y], SENT, RIGHT + zp, chip(ty, tz)).start()
    pltpu.make_async_copy(send_r.at[me], recv_r.at[zp, zb, y], sems.at[RIGHT + zp]).start()
    for dy, dz in ring:
        ty, tz = lax.rem(y + dy, NY), lax.rem(z + dz, NZ)
        remote(send_l.at[tz * NY + ty], recv_l.at[z, y], SENT + 1, LEFT, chip(ty, tz)).start()
    pltpu.make_async_copy(send_l.at[me], recv_l.at[z, y], sems.at[LEFT]).start()

    def merge(tiles):
        tiles = [tile.astype(F32) for tile in tiles]
        made = []
        for b in range(4):
            moved = [t if s == b else pltpu.roll(t, (s - b) % 4 * 32, 1) for s, t in enumerate(tiles)]
            made.append(jnp.where(low, jnp.where(even, moved[0], moved[1]), jnp.where(even, moved[2], moved[3])))
        return [jnp.concatenate(made[c * 2 : c * 2 + 2], axis=0).astype(BF16) for c in range(2)]

    def spread(p):
        wait_bytes(recv_r.at[p], sems.at[RIGHT + p])
        for b in range(2):
            for q in range(2):
                both = merge([recv_r[p, b, 4 * q + s] for s in range(4)])
                for c in range(2):
                    right[p, xh, b, xl, c, :, q * 128 : (q + 1) * 128] = both[c]
        own = right.at[p, xh, :, xl]
        for d, there in along:
            remote(own, own, SENT + 2, GATHER + 3 * p + d - 1, there).start()

    def contract(p):
        for d, _ in along:
            source = lax.rem(x + NX - d, NX)
            wait_bytes(right.at[p, lax.div(source, 2), :, lax.rem(source, 2)], sems.at[GATHER + 3 * p + d - 1])
        one, two = [
            nt(left[c].reshape(128, 256), right[p, :, :, :, c].reshape(128, 256)) for c in range(2)
        ]
        first = lax.broadcasted_iota(jnp.int32, (128, 128), 1) < 64
        part[p, 0] = jnp.where(first, one, half_roll(two))
        part[p, 1] = jnp.where(first, half_roll(one), two)
        remote(part.at[p, 1 - core], other.at[p], SENT + 3, ADD + p, beside).start()

    def finish(p):
        wait_bytes(other.at[p], sems.at[ADD + p])
        for zz in range(8):
            top, low_rows = slice(zz * 16, zz * 16 + 8), slice(zz * 16 + 8, zz * 16 + 16)
            one = part[p, core, top, :] + other[p, top, :]
            two = part[p, core, low_rows, :] + other[p, low_rows, :]
            back[p, 0, zz] = jnp.where(even, one, pltpu.roll(two, 32, 1)).astype(BF16)
            back[p, 1, zz] = jnp.where(even, pltpu.roll(one, 96, 1), two).astype(BF16)

        def give_back(b, tz):
            remote(back.at[p, b, tz], home.at[me], SENT + 4, BACK, chip(p * 2 + b, tz)).start()

        for dz in (4, 3, 5, 2, 6, 1, 7):
            for b in range(2):
                give_back(b, lax.rem(z + dz, NZ))
        for b in range(2):

            @pl.when(p * 2 + b != y)
            def _(b=b):
                give_back(b, z)

    c0, c1, c2, c3 = ORDER
    for p in ORDER:
        spread(p)
    wait_bytes(recv_l, sems.at[LEFT])
    for zz in range(8):
        for q in range(2):
            both = merge([recv_l[zz, 4 * q + s] for s in range(4)])
            for c in range(2):
                left[c, zz, :, q * 128 : (q + 1) * 128] = both[c]
    contract(c0)
    contract(c1)
    finish(c0)
    contract(c2)
    finish(c1)
    contract(c3)
    finish(c2)
    finish(c3)
    pltpu.make_async_copy(back.at[lax.div(y, 2), lax.rem(y, 2), z], home.at[me], sems.at[BACK]).start()
    wait_bytes(home, sems.at[BACK])

    final[...] = home[...].reshape(512, 128).astype(F32)
    for t in range(0, 8, 2):
        one, two = final[pl.ds(t, 64, stride=8), :], final[pl.ds(t + 1, 64, stride=8), :]
        mixed = jnp.concatenate(
            [jnp.where(wide_low, one, half_roll(two)), jnp.where(wide_low, half_roll(one), two)], axis=0
        )
        mean = jnp.mean(mixed, axis=0, keepdims=True)
        centered = mixed - mean
        var = jnp.mean(centered * centered, axis=0, keepdims=True)
        mixed_norm = (centered * lax.rsqrt(var + EPS) * gain).astype(BF16)
        rows = lax.dot_general(
            mixed_norm, wout[...], (((0,), (0,)), ((), ())), preferred_element_type=F32
        )
        for n, i in enumerate((t, 8 + t, t + 1, 9 + t)):
            out[i] = (gate[i] * rows[n * 32 : (n + 1) * 32]).astype(BF16)

    wait_bytes(send_r.at[pl.ds(0, NG - 1)], sems.at[SENT])
    wait_bytes(send_l.at[pl.ds(0, NG - 1)], sems.at[SENT + 1])
    for p in range(3):
        wait_bytes(right.at[p], sems.at[SENT + 2])
    wait_bytes(other, sems.at[SENT + 3])
    wait_bytes(send_l.at[pl.ds(0, NG - 1)], sems.at[SENT + 4])


def on_device(pair, gain_in, w_in, w_gate, w_out, gain_mid, chain_len, allowed):
    operands = (pair, gain_in.reshape(1, 128), w_in, w_gate, w_out, gain_mid.reshape(1, 128))
    scalars = (chain_len, allowed)
    return pl.pallas_call(
        kernel,
        out_shape=jax.ShapeDtypeStruct(pair.shape, pair.dtype),
        in_specs=[pl.BlockSpec(memory_space=pl.ANY)] * 8,
        out_specs=pl.BlockSpec(memory_space=pltpu.VMEM),
        scratch_shapes=[
            *[pltpu.VMEM(a.shape, a.dtype) for a in operands],
            *[pltpu.SMEM(a.shape, a.dtype) for a in scalars],
            pltpu.VMEM((16, 32, 128), F32),
            pltpu.VMEM((512, 128), BF16),
            pltpu.VMEM((512, 128), F32),
            pltpu.VMEM((NG, 8, 128), BF16),
            pltpu.VMEM((NG, 8, 128), BF16),
            pltpu.VMEM((4, 2, NY, 8, 128), BF16),
            pltpu.VMEM((NZ, NY, 8, 128), BF16),
            pltpu.VMEM((2, NZ, 16, 256), BF16),
            pltpu.VMEM((4, 2, 2, 2, 2, 16, 256), BF16),
            pltpu.VMEM((4, 2, 128, 128), F32),
            pltpu.VMEM((4, 128, 128), F32),
            pltpu.VMEM((4, 2, NZ, 8, 128), BF16),
            pltpu.VMEM((NG, 8, 128), BF16),
            pltpu.VMEM((512, 128), F32),
            pltpu.SemaphoreType.DMA((LOAD + 8,)),
        ],
        compiler_params=pltpu.CompilerParams(
            collective_id=0, has_side_effects=True, vmem_limit_bytes=32 * 2**20
        ),
    )(*[pltpu.with_memory_space_constraint(a, pltpu.HBM) for a in (*operands, *scalars)])


def solution(mesh):
    return jax.shard_map(
        on_device,
        mesh=mesh,
        in_specs=(P("row", "col", None), P(), P(), P(), P(), P(), P(), P()),
        out_specs=P("row", "col", None),
        check_vma=False,
    )
```

```python
import jax
import jax.numpy as jnp
from jax import lax
from jax.experimental import pallas as pl
from jax.experimental.pallas import tpu as pltpu
from jax.sharding import PartitionSpec as P

MESH = pl.DeviceIdType.MESH
F32, BF16 = jnp.float32, jnp.bfloat16
NX, NY, NZ = 4, 8, 8
NG = NY * NZ
ORDER = (0, 1, 3, 2)
EPS = 1e-5
RIGHT, LEFT, GATHER, ADD, BACK, SENT, LOAD = 0, 4, 5, 17, 21, 22, 27


def nt(a, b):
    return lax.dot_general(a, b, (((1,), (1,)), ((), ())), preferred_element_type=F32)


def sigmoid(v):
    return 1.0 / (1.0 + jnp.exp(-v))


def wait_bytes(ref, sem):
    pltpu.make_async_copy(ref, ref, sem).wait()


def kernel(
    pair_hbm, gin_hbm, win_hbm, wgate_hbm, wout_hbm, gmid_hbm, len_hbm, allowed_hbm, out,
    pair, gin, win, wgate, wout, gmid, chain_len, allowed,
    gate, wt, stage, send_r, send_l, recv_r, recv_l, left, right, part, other, back, home, final, sems,
):
    row, col = lax.axis_index("row"), lax.axis_index("col")
    z, x = lax.div(row, NX), lax.rem(row, NX)
    y, core = lax.div(col, 2), lax.rem(col, 2)
    zp, zb = lax.div(z, 2), lax.rem(z, 2)
    xh, xl = lax.div(x, 2), lax.rem(x, 2)
    me = z * NY + y

    def chip(ty, tz):
        return (tz * NX + x, ty * 2 + core)

    def remote(src, dst, sent, arrived, there):
        return pltpu.make_async_remote_copy(
            src, dst, sems.at[sent], sems.at[arrived], device_id=there, device_id_type=MESH
        )

    beside = (row, col + 1 - 2 * core)
    along = [(d, (z * NX + lax.rem(x + d, NX), col)) for d in (2, 1, 3)]

    loads = [
        pltpu.make_async_copy(src, dst, sems.at[LOAD + n])
        for n, (src, dst) in enumerate(
            [(pair_hbm, pair), (gin_hbm, gin), (win_hbm, win), (wgate_hbm, wgate), (wout_hbm, wout),
             (gmid_hbm, gmid), (len_hbm, chain_len), (allowed_hbm, allowed)]
        )
    ]
    for load in loads:
        load.start()

    ring = [(dy, dz) for dy in range(NY) for dz in range(NZ) if dy or dz]
    ring.sort(key=lambda o: -min(o[0], NY - o[0]) - min(o[1], NZ - o[1]))
    barrier = pltpu.get_barrier_semaphore()
    for dy, dz in ring:
        there = chip(lax.rem(y + dy, NY), lax.rem(z + dz, NZ))
        pl.semaphore_signal(barrier, inc=1, device_id=there, device_id_type=MESH)
    for there in [beside] + [there for _, there in along]:
        pl.semaphore_signal(barrier, inc=1, device_id=there, device_id_type=MESH)

    lane = lax.broadcasted_iota(jnp.int32, (8, 128), 1)
    low = lane < 64
    lane32 = jnp.where(low, lane, lane - 64)
    even = lane32 < 32
    lane32 = jnp.where(even, lane32, lane32 - 32)

    def half_roll(v):
        return pltpu.roll(v, 64, 1)

    loads[0].wait()
    loads[1].wait()
    values = pair[...].reshape(512, 128).astype(F32)
    mean = jnp.mean(values, axis=1, keepdims=True)
    centered = values - mean
    var = jnp.mean(centered * centered, axis=1, keepdims=True)
    normed = (centered * lax.rsqrt(var + EPS) * gin[...]).astype(BF16)
    loads[2].wait()
    for b in range(4):
        wt[b * 128 : (b + 1) * 128, :] = win[:, b * 128 : (b + 1) * 128].astype(F32).T.astype(BF16)
    for load in loads[3:]:
        load.wait()

    column = col * 32 + lane32
    chain_row, chain_col, end = jnp.int32(0), jnp.zeros((8, 128), jnp.int32), jnp.int32(0)
    for c in range(3):
        end = end + chain_len[c]
        chain_row = chain_row + jnp.where(row >= end, 1, 0)
        chain_col = chain_col + jnp.where(column >= end * 16, 1, 0)
    mask = jnp.zeros((8, 128), F32)
    for b in range(4):
        pick = jnp.int32(0)
        for a in range(4):
            pick = jnp.where(chain_row == a, allowed[a, b], pick)
        mask = jnp.where(chain_col == b, pick.astype(F32), mask)
    mask = mask[0:1]

    wide_low = lax.broadcasted_iota(jnp.int32, (64, 128), 1) < 64

    def project(first, store):
        weights = wt[first * 128 : (first + 2) * 128, :]
        for t in range(0, 8, 2):
            four = [normed[i * 32 : (i + 1) * 32] for i in (t, 8 + t, t + 1, 9 + t)]
            proj = nt(weights, jnp.concatenate(four, axis=0))
            gated = sigmoid(proj[:128]) * proj[128:] * mask
            one, two = gated[:64], gated[64:]
            stage[pl.ds(t, 64, stride=8), :] = jnp.where(wide_low, one, half_roll(two))
            stage[pl.ds(t + 1, 64, stride=8), :] = jnp.where(wide_low, half_roll(one), two)
        store[...] = stage[...].reshape(64, 8, 128).astype(BF16)

    project(2, send_r)
    project(0, send_l)
    gate[...] = sigmoid(jnp.dot(normed, wgate[...], preferred_element_type=F32)).reshape(16, 32, 128)
    gain = jnp.broadcast_to(gmid[...], (128, 128)).T

    pl.semaphore_wait(barrier, NG + 3)
    for dy, dz in ring:
        ty, tz = lax.rem(y + dy, NY), lax.rem(z + dz, NZ)
        remote(send_r.at[tz * NY + ty], recv_r.at[zp, zb, y], SENT, RIGHT + zp, chip(ty, tz)).start()
    pltpu.make_async_copy(send_r.at[me], recv_r.at[zp, zb, y], sems.at[RIGHT + zp]).start()
    for dy, dz in ring:
        ty, tz = lax.rem(y + dy, NY), lax.rem(z + dz, NZ)
        remote(send_l.at[tz * NY + ty], recv_l.at[z, y], SENT + 1, LEFT, chip(ty, tz)).start()
    pltpu.make_async_copy(send_l.at[me], recv_l.at[z, y], sems.at[LEFT]).start()

    def merge(tiles):
        tiles = [tile.astype(F32) for tile in tiles]
        made = []
        for b in range(4):
            moved = [t if s == b else pltpu.roll(t, (s - b) % 4 * 32, 1) for s, t in enumerate(tiles)]
            made.append(jnp.where(low, jnp.where(even, moved[0], moved[1]), jnp.where(even, moved[2], moved[3])))
        return [jnp.concatenate(made[c * 2 : c * 2 + 2], axis=0).astype(BF16) for c in range(2)]

    def spread(p):
        wait_bytes(recv_r.at[p], sems.at[RIGHT + p])
        for b in range(2):
            for q in range(2):
                both = merge([recv_r[p, b, 4 * q + s] for s in range(4)])
                for c in range(2):
                    right[p, xh, b, xl, c, :, q * 128 : (q + 1) * 128] = both[c]
            own = right.at[p, xh, b, xl]
            for d, there in along:
                remote(own, own, SENT + 2, GATHER + 3 * p + d - 1, there).start()

    def contract(p):
        for half in (1 - core, core):
            for e in range(2):
                d = lax.rem(x - (2 * half + e) + NX, NX)

                @pl.when(d > 0)
                def _(half=half, e=e, d=d):
                    wait_bytes(right.at[p, half, :, e], sems.at[GATHER + 3 * p + d - 1])

            both = [nt(left[c].reshape(128, 256), right[p, half, :, :, c].reshape(64, 256)) for c in range(2)]
            part[p, half] = jnp.concatenate(both, axis=1)
            if half is not core:
                remote(part.at[p, half], other.at[p], SENT + 3, ADD + p, beside).start()

    def finish(p):
        wait_bytes(other.at[p], sems.at[ADD + p])
        for zz in range(8):
            top, low_rows = slice(zz * 16, zz * 16 + 8), slice(zz * 16 + 8, zz * 16 + 16)
            one = part[p, core, top, :] + other[p, top, :]
            two = part[p, core, low_rows, :] + other[p, low_rows, :]
            back[p, 0, zz] = jnp.where(even, one, pltpu.roll(two, 32, 1)).astype(BF16)
            back[p, 1, zz] = jnp.where(even, pltpu.roll(one, 96, 1), two).astype(BF16)

        def give_back(b, tz):
            remote(back.at[p, b, tz], home.at[me], SENT + 4, BACK, chip(p * 2 + b, tz)).start()

        for dz in (4, 3, 5, 2, 6, 1, 7):
            for b in range(2):
                give_back(b, lax.rem(z + dz, NZ))
        for b in range(2):

            @pl.when(p * 2 + b != y)
            def _(b=b):
                give_back(b, z)

    c0, c1, c2, c3 = ORDER
    for p in ORDER:
        spread(p)
    wait_bytes(recv_l, sems.at[LEFT])
    for zz in range(8):
        for q in range(2):
            both = merge([recv_l[zz, 4 * q + s] for s in range(4)])
            for c in range(2):
                left[c, zz, :, q * 128 : (q + 1) * 128] = both[c]
    contract(c0)
    contract(c1)
    finish(c0)
    contract(c2)
    finish(c1)
    contract(c3)
    finish(c2)
    finish(c3)
    pltpu.make_async_copy(back.at[lax.div(y, 2), lax.rem(y, 2), z], home.at[me], sems.at[BACK]).start()
    wait_bytes(home, sems.at[BACK])

    final[...] = home[...].reshape(512, 128).astype(F32)
    for t in range(0, 8, 2):
        one, two = final[pl.ds(t, 64, stride=8), :], final[pl.ds(t + 1, 64, stride=8), :]
        mixed = jnp.concatenate(
            [jnp.where(wide_low, one, half_roll(two)), jnp.where(wide_low, half_roll(one), two)], axis=0
        )
        mean = jnp.mean(mixed, axis=0, keepdims=True)
        centered = mixed - mean
        var = jnp.mean(centered * centered, axis=0, keepdims=True)
        mixed_norm = (centered * lax.rsqrt(var + EPS) * gain).astype(BF16)
        rows = lax.dot_general(
            mixed_norm, wout[...], (((0,), (0,)), ((), ())), preferred_element_type=F32
        )
        for n, i in enumerate((t, 8 + t, t + 1, 9 + t)):
            out[i] = (gate[i] * rows[n * 32 : (n + 1) * 32]).astype(BF16)

    wait_bytes(send_r.at[pl.ds(0, NG - 1)], sems.at[SENT])
    wait_bytes(send_l.at[pl.ds(0, NG - 1)], sems.at[SENT + 1])
    for p in range(3):
        wait_bytes(right.at[p], sems.at[SENT + 2])
    wait_bytes(other, sems.at[SENT + 3])
    wait_bytes(send_l.at[pl.ds(0, NG - 1)], sems.at[SENT + 4])


def on_device(pair, gain_in, w_in, w_gate, w_out, gain_mid, chain_len, allowed):
    operands = (pair, gain_in.reshape(1, 128), w_in, w_gate, w_out, gain_mid.reshape(1, 128))
    scalars = (chain_len, allowed)
    return pl.pallas_call(
        kernel,
        out_shape=jax.ShapeDtypeStruct(pair.shape, pair.dtype),
        in_specs=[pl.BlockSpec(memory_space=pl.ANY)] * 8,
        out_specs=pl.BlockSpec(memory_space=pltpu.VMEM),
        scratch_shapes=[
            *[pltpu.VMEM(a.shape, a.dtype) for a in operands],
            *[pltpu.SMEM(a.shape, a.dtype) for a in scalars],
            pltpu.VMEM((16, 32, 128), F32),
            pltpu.VMEM((512, 128), BF16),
            pltpu.VMEM((512, 128), F32),
            pltpu.VMEM((NG, 8, 128), BF16),
            pltpu.VMEM((NG, 8, 128), BF16),
            pltpu.VMEM((4, 2, NY, 8, 128), BF16),
            pltpu.VMEM((NZ, NY, 8, 128), BF16),
            pltpu.VMEM((2, NZ, 16, 256), BF16),
            pltpu.VMEM((4, 2, 2, 2, 2, 16, 256), BF16),
            pltpu.VMEM((4, 2, 128, 128), F32),
            pltpu.VMEM((4, 128, 128), F32),
            pltpu.VMEM((4, 2, NZ, 8, 128), BF16),
            pltpu.VMEM((NG, 8, 128), BF16),
            pltpu.VMEM((512, 128), F32),
            pltpu.SemaphoreType.DMA((LOAD + 8,)),
        ],
        compiler_params=pltpu.CompilerParams(
            collective_id=0, has_side_effects=True, vmem_limit_bytes=32 * 2**20
        ),
    )(*[pltpu.with_memory_space_constraint(a, pltpu.HBM) for a in (*operands, *scalars)])


def solution(mesh):
    return jax.shard_map(
        on_device,
        mesh=mesh,
        in_specs=(P("row", "col", None), P(), P(), P(), P(), P(), P(), P()),
        out_specs=P("row", "col", None),
        check_vma=False,
    )
```
